32 devices in a mesh: dp: 16 (over z, y, core), tensor: 2 (over x).
Axes of the slice: x: 2, y: 2, z: 4, core: 2. Of those that a mesh axis runs over, the one named last changes fastest.
Arguments:
- inputs: bfloat16 [48, 577, 1024], P('dp'), may hold values from -6 to 6
- cotangent: bfloat16 [48, 577, 1024], P('dp'), may hold values from -6 to 6
- image_flags: int32 [48], P('dp'), may hold values 0 or 1
- qkv_master: float32 [3, 1024, 1024], P(None, 'dp', 'tensor')
- qkv_first: float32 [3, 1024, 1024], P(None, 'dp', 'tensor')
- qkv_second: float32 [3, 1024, 1024], P(None, 'dp', 'tensor')
- out_master: float32 [1024, 1024], P(('tensor', 'dp')), may hold values from -0.5 to 0.5
- out_first: float32 [1024, 1024], P(('tensor', 'dp'))
- out_second: float32 [1024, 1024], P(('tensor', 'dp'))
- up_master: float32 [1024, 4, 1024], P('dp', None, 'tensor'), may hold values from -0.1875 to 0.1875
- up_first: float32 [1024, 4, 1024], P('dp', None, 'tensor')
- up_second: float32 [1024, 4, 1024], P('dp', None, 'tensor')
- down_master: float32 [4, 1024, 1024], P(None, ('tensor', 'dp')), may hold values from -0.125 to 0.125
- down_first: float32 [4, 1024, 1024], P(None, ('tensor', 'dp'))
- down_second: float32 [4, 1024, 1024], P(None, ('tensor', 'dp'))
- norm_master: float32 [6, 1024], P(None, 'dp')
- norm_first: float32 [6, 1024], P(None, 'dp')
- norm_second: float32 [6, 1024], P(None, 'dp')
- inner_master: float32 [6, 1024], P(None, ('tensor', 'dp'))
- inner_first: float32 [6, 1024], P(None, ('tensor', 'dp'))
- inner_second: float32 [6, 1024], P(None, ('tensor', 'dp'))
Outputs:
- outputs: bfloat16 [48, 577, 1024], P('dp')
- input_grad: float32 [48, 577, 1024], P('dp')
- qkv_master_new: float32 [3, 1024, 1024], P(None, 'dp', 'tensor')
- qkv_first_new: float32 [3, 1024, 1024], P(None, 'dp', 'tensor')
- qkv_second_new: float32 [3, 1024, 1024], P(None, 'dp', 'tensor')
- qkv_copy: bfloat16 [3, 1024, 1024], P(None, 'dp', 'tensor')
- out_master_new: float32 [1024, 1024], P(('tensor', 'dp'))
- out_first_new: float32 [1024, 1024], P(('tensor', 'dp'))
- out_second_new: float32 [1024, 1024], P(('tensor', 'dp'))
- out_copy: bfloat16 [1024, 1024], P(('tensor', 'dp'))
- up_master_new: float32 [1024, 4, 1024], P('dp', None, 'tensor')
- up_first_new: float32 [1024, 4, 1024], P('dp', None, 'tensor')
- up_second_new: float32 [1024, 4, 1024], P('dp', None, 'tensor')
- up_copy: bfloat16 [1024, 4, 1024], P('dp', None, 'tensor')
- down_master_new: float32 [4, 1024, 1024], P(None, ('tensor', 'dp'))
- down_first_new: float32 [4, 1024, 1024], P(None, ('tensor', 'dp'))
- down_second_new: float32 [4, 1024, 1024], P(None, ('tensor', 'dp'))
- down_copy: bfloat16 [4, 1024, 1024], P(None, ('tensor', 'dp'))
- norm_master_new: float32 [6, 1024], P(None, 'dp')
- norm_first_new: float32 [6, 1024], P(None, 'dp')
- norm_second_new: float32 [6, 1024], P(None, 'dp')
- norm_copy: bfloat16 [6, 1024], P(None, 'dp')
- inner_master_new: float32 [6, 1024], P(None, ('tensor', 'dp'))
- inner_first_new: float32 [6, 1024], P(None, ('tensor', 'dp'))
- inner_second_new: float32 [6, 1024], P(None, ('tensor', 'dp'))
- inner_copy: bfloat16 [6, 1024], P(None, ('tensor', 'dp'))
The draws below stay inside these ranges and needn't reach their ends.
All inputs are finite; a program needn't handle non-finite values. No bound on the sum of `image_flags` on one device may be relied on, other than what follows from the above.
Results may differ from the reference program's by a relative error of at most 0.035.
Values may be sent and summed in bfloat16 or wider, within the bound.
No kernel may reach another device: no remote copies, remote signals or barrier semaphores. Data moves between devices by JAX's collectives and lax.ppermute only.
A program may use at most 256 MiB of HBM per device.

```python
import math
import jax
import jax.numpy as jnp
from jax import lax

D = 1024
HEADS = 16
HD = 64
FF = 4096
SEQ = 577
STEP = 5
IMAGES = 48
N_TENSOR = 2


def grad_size(scales):
    return jnp.asarray(scales, jnp.float32) * math.sqrt(IMAGES * SEQ * 0.75)


def first_moment(key, dims_shape, scales):
    noise = jax.random.truncated_normal(key, -3.0, 3.0, dims_shape, jnp.float32)
    return grad_size(scales) * noise


def second_moment(key, dims_shape, scales):
    factor = jnp.exp(jax.random.uniform(key, dims_shape, jnp.float32, 0.0, math.log(4.0)))
    return factor * grad_size(scales) ** 2


def qkv_scales():
    return jnp.array([0.9, 1.8, 0.9], jnp.float32).reshape(3, 1, 1)


def norm_scales():
    return jnp.array([2.7, 2.7, 0.42, 0.42, 1.0, 1.0], jnp.float32).reshape(6, 1)


def inner_scales():
    unit_rows = FF // D
    return jnp.concatenate([jnp.full((2, 1), 0.9, jnp.float32), jnp.full((unit_rows, 1), 0.42, jnp.float32)])


def draw_qkv_master(key, part):
    key = jax.random.fold_in(key, 1)
    noise = jax.random.truncated_normal(key, -3.0, 3.0, (3, D, D), jnp.float32)
    return jnp.array([2.0, 1.0, 1.0], jnp.float32).reshape(3, 1, 1) / math.sqrt(D) * noise


def draw_qkv_first(key, part):
    key = jax.random.fold_in(key, 2)
    return first_moment(key, (3, D, D), qkv_scales())


def draw_qkv_second(key, part):
    key = jax.random.fold_in(key, 3)
    return second_moment(key, (3, D, D), qkv_scales())


def draw_out_first(key, part):
    key = jax.random.fold_in(key, 4)
    return first_moment(key, (D, D), 0.35)


def draw_out_second(key, part):
    key = jax.random.fold_in(key, 5)
    return second_moment(key, (D, D), 0.35)


def draw_up_first(key, part):
    key = jax.random.fold_in(key, 6)
    return first_moment(key, (D, FF // D, D), 0.42)


def draw_up_second(key, part):
    key = jax.random.fold_in(key, 7)
    return second_moment(key, (D, FF // D, D), 0.42)


def draw_down_first(key, part):
    key = jax.random.fold_in(key, 8)
    return first_moment(key, (FF // D, D, D), 0.6)


def draw_down_second(key, part):
    key = jax.random.fold_in(key, 9)
    return second_moment(key, (FF // D, D, D), 0.6)


def draw_norm_master(key, part):
    key = jax.random.fold_in(key, 10)
    noise = jax.random.truncated_normal(key, -3.0, 3.0, (6, D), jnp.float32)
    offset = jnp.array([1.0, 0.0, 1.0, 0.0, 0.0, 0.0], jnp.float32).reshape(6, 1)
    spread = jnp.array([0.1, 0.2, 0.1, 0.2, 0.2, 0.2], jnp.float32).reshape(6, 1)
    return offset + spread * noise


def draw_norm_first(key, part):
    key = jax.random.fold_in(key, 11)
    return first_moment(key, (6, D), norm_scales())


def draw_norm_second(key, part):
    key = jax.random.fold_in(key, 12)
    return second_moment(key, (6, D), norm_scales())


def draw_inner_master(key, part):
    key = jax.random.fold_in(key, 13)
    unit_rows = FF // D
    noise = jax.random.truncated_normal(key, -3.0, 3.0, (2 + unit_rows, D), jnp.float32)
    spread = jnp.concatenate([jnp.full((2, 1), 0.2, jnp.float32), jnp.full((unit_rows, 1), 0.3, jnp.float32)])
    return spread * noise


def draw_inner_first(key, part):
    key = jax.random.fold_in(key, 14)
    return first_moment(key, (2 + FF // D, D), inner_scales())


def draw_inner_second(key, part):
    key = jax.random.fold_in(key, 15)
    return second_moment(key, (2 + FF // D, D), inner_scales())


def with_ends(entries, key, low, top_value):
    shape = entries.shape
    spot = [jax.random.randint(jax.random.fold_in(key, axis), (), 0, shape[axis]) for axis in range(len(shape))]
    entries = entries.at[tuple(spot)].set(low)
    longest = shape.index(max(shape))
    spot[longest] = (spot[longest] + 1) % shape[longest]
    return entries.at[tuple(spot)].set(top_value)


def block_levels(own_key, dims, pieces, low, top_value):
    level = 1.0
    for axis_at, parts in pieces:
        draws = jax.random.uniform(jax.random.fold_in(jax.random.fold_in(own_key, 6), axis_at), (parts,), jnp.float32, low / len(pieces), top_value / len(pieces))
        level = level * jnp.repeat(jnp.exp(draws), dims[axis_at] // parts).reshape((-1,) + (1,) * (len(dims) - 1 - axis_at))
    return level


def gaussian(own_key, shape, scale, bound, cuts=(), held_as=jnp.bfloat16):
    factor_of = block_levels(own_key, shape, cuts, -0.22, 0.18) if cuts else 1.0
    drawn = jax.random.normal(own_key, shape, jnp.float32) * scale * factor_of
    return jnp.minimum(jnp.maximum(drawn, -bound), bound).astype(held_as)


def setup_inputs(seed: int = 0) -> dict:
    seeds = jax.random.split(jax.random.key(seed), 22)
    return {
        "inputs": gaussian(seeds[0], (IMAGES, SEQ, D), 1.0, 6.0, ((0, 16),)),
        "cotangent": gaussian(seeds[1], (IMAGES, SEQ, D), 1.0, 6.0, ((0, 16),)),
        "image_flags": with_ends((jax.random.randint(seeds[2], (IMAGES,), 0, 4) < 3).astype(jnp.int32), jax.random.fold_in(seeds[2], 1), 0, 1),
        "qkv_master": draw_qkv_master(jax.random.fold_in(seeds[21], 71), 0),
        "qkv_first": draw_qkv_first(jax.random.fold_in(seeds[21], 71), 0),
        "qkv_second": draw_qkv_second(jax.random.fold_in(seeds[21], 71), 0),
        "out_master": gaussian(seeds[6], (D, D), (D // 8) ** -0.5, 0.5, ((0, 32),), jnp.float32),
        "out_first": draw_out_first(jax.random.fold_in(seeds[21], 71), 0),
        "out_second": draw_out_second(jax.random.fold_in(seeds[21], 71), 0),
        "up_master": gaussian(seeds[9], (D, FF // D, D), D ** -0.5, 0.1875, ((0, 16), (2, 2)), jnp.float32),
        "up_first": draw_up_first(jax.random.fold_in(seeds[21], 71), 0),
        "up_second": draw_up_second(jax.random.fold_in(seeds[21], 71), 0),
        "down_master": gaussian(seeds[12], (FF // D, D, D), (FF // 2) ** -0.5, 0.125, ((1, 32),), jnp.float32),
        "down_first": draw_down_first(jax.random.fold_in(seeds[21], 71), 0),
        "down_second": draw_down_second(jax.random.fold_in(seeds[21], 71), 0),
        "norm_master": draw_norm_master(jax.random.fold_in(seeds[21], 71), 0),
        "norm_first": draw_norm_first(jax.random.fold_in(seeds[21], 71), 0),
        "norm_second": draw_norm_second(jax.random.fold_in(seeds[21], 71), 0),
        "inner_master": draw_inner_master(jax.random.fold_in(seeds[21], 71), 0),
        "inner_first": draw_inner_first(jax.random.fold_in(seeds[21], 71), 0),
        "inner_second": draw_inner_second(jax.random.fold_in(seeds[21], 71), 0),
    }


EPSILON = 1e-05
BETA_FIRST = 0.5
BETA_SECOND = 0.5
WEIGHT_DECAY = 0.1
ADAM_EPS = 1e-08
LEARN_RATES = (0.03, 0.1, 0.03, 0.015, 0.2, 0.2)

@jax.custom_vjp
def low(v):
    return lax.optimization_barrier(v.astype(jnp.bfloat16)).astype(jnp.float32)

@jax.custom_vjp
def low_back(v):
    return v

def low_keep(v):
    return (low(v), None)

def low_pass(kept, grad):
    return (grad,)

def back_keep(v):
    return (v, None)

def back_low(kept, grad):
    return (low(grad),)
low.defvjp(low_keep, low_pass)
low_back.defvjp(back_keep, back_low)

def dot_high(form, left_side, right_side):
    return jnp.einsum(form, left_side, right_side, precision=lax.Precision.HIGHEST)

def layer_norm(values, gain_vec, shift_vec):
    center = values - lax.optimization_barrier(jnp.mean(values, axis=-1, keepdims=True))
    normed = center * lax.rsqrt(lax.optimization_barrier(jnp.mean(center * center, axis=-1, keepdims=True)) + EPSILON)
    return normed * gain_vec + shift_vec

def group_copies(values, groups):
    return jnp.stack([low_back(values) for index in range(groups)])

def forward_one(params, image):
    qkv_used, out_used, up_used, down_used, norm_used, inner_used = params
    length = image.shape[0]
    groups = N_TENSOR
    group_width = D // groups
    attn_in = low(layer_norm(image, norm_used[0], norm_used[1]))
    attn_copies = group_copies(attn_in, groups)
    project = dot_high('gsd,cdgk->csgk', attn_copies, qkv_used.reshape(3, D, groups, group_width)).reshape(3, length, D)
    queries = low(low_back(project[0] + inner_used[0])).reshape(length, HEADS, HD)
    key_vecs = low(low_back(project[1])).reshape(length, HEADS, HD)
    values = low(low_back(project[2] + inner_used[1])).reshape(length, HEADS, HD)
    scores = low_back(dot_high('shd,thd->hst', queries, key_vecs) * HD ** (-0.5))
    probs_full = jax.nn.softmax(scores, axis=-1)
    mixed = dot_high('hst,thd->shd', low(probs_full), values).reshape(length, D)
    mixed = low(low_back(mixed))
    attn_part = dot_high('sgk,gkd->gsd', mixed.reshape(length, groups, group_width), out_used.reshape(groups, group_width, D))
    attn_out = low_back(lax.optimization_barrier(jnp.sum(low(attn_part), axis=0)) + norm_used[4])
    hidden = image + attn_out
    mlp_in = low(layer_norm(hidden, norm_used[2], norm_used[3]))
    unit_rows = up_used.shape[1]
    mlp_copies = group_copies(mlp_in, groups)
    pre_lin = dot_high('gsd,drgk->srgk', mlp_copies, up_used.reshape(D, unit_rows, groups, group_width)).reshape(length, unit_rows, D)
    pre_act = low_back(pre_lin + inner_used[2:])
    act_vals = low(pre_act * jax.nn.sigmoid(1.702 * pre_act))
    mlp_part = dot_high('srgk,rgkd->gsd', act_vals.reshape(length, unit_rows, groups, group_width), down_used.reshape(unit_rows, groups, group_width, D))
    mlp_out = low_back(lax.optimization_barrier(jnp.sum(low(mlp_part), axis=0)) + norm_used[5])
    return hidden + mlp_out

def adam_update(master, moment_one, moment_two, gradient, learn_rate):
    new_first = BETA_FIRST * moment_one + (1.0 - BETA_FIRST) * gradient
    new_second = BETA_SECOND * moment_two + (1.0 - BETA_SECOND) * gradient * gradient
    fixed_first = new_first / (1.0 - BETA_FIRST ** STEP)
    fixed_second = new_second / (1.0 - BETA_SECOND ** STEP)
    new_master = master - learn_rate * (fixed_first / (jnp.sqrt(fixed_second) + ADAM_EPS) + WEIGHT_DECAY * master)
    return (new_master, new_first, new_second, new_master.astype(jnp.bfloat16))

def reference(inputs, cotangent, image_flags, qkv_master, qkv_first, qkv_second, out_master, out_first, out_second, up_master, up_first, up_second, down_master, down_first, down_second, norm_master, norm_first, norm_second, inner_master, inner_first, inner_second):
    masters = (qkv_master, out_master, up_master, down_master, norm_master, inner_master)
    params = tuple((lax.optimization_barrier(master.astype(jnp.bfloat16)).astype(jnp.float32) for master in masters))
    flagged = cotangent.astype(jnp.float32) * image_flags.astype(jnp.float32)[:, None, None]

    def one_image(running, image_pair):
        image, grad_out = image_pair
        result, pullback = jax.vjp(forward_one, params, image)
        param_grads, image_grad = pullback(grad_out)
        return (jax.tree.map(jnp.add, running, param_grads), (result.astype(jnp.bfloat16), image_grad))
    zero_grads = tuple((jnp.zeros(used.shape, jnp.float32) for used in params))
    totals, (outputs, input_grad) = lax.scan(one_image, zero_grads, (inputs.astype(jnp.float32), flagged))
    qkv_new = adam_update(qkv_master, qkv_first, qkv_second, totals[0], LEARN_RATES[0])
    out_new = adam_update(out_master, out_first, out_second, totals[1], LEARN_RATES[1])
    up_new = adam_update(up_master, up_first, up_second, totals[2], LEARN_RATES[2])
    down_new = adam_update(down_master, down_first, down_second, totals[3], LEARN_RATES[3])
    norm_new = adam_update(norm_master, norm_first, norm_second, totals[4], LEARN_RATES[4])
    inner_new = adam_update(inner_master, inner_first, inner_second, totals[5], LEARN_RATES[5])
    return (outputs, input_grad, qkv_new[0], qkv_new[1], qkv_new[2], qkv_new[3], out_new[0], out_new[1], out_new[2], out_new[3], up_new[0], up_new[1], up_new[2], up_new[3], down_new[0], down_new[1], down_new[2], down_new[3], norm_new[0], norm_new[1], norm_new[2], norm_new[3], inner_new[0], inner_new[1], inner_new[2], inner_new[3])
```

```python
import jax
import jax.numpy as jnp
from jax import lax
from jax.sharding import PartitionSpec as P

HD = 64
STEP = 5


EPSILON = 1e-05
BETA_FIRST = 0.5
BETA_SECOND = 0.5
WEIGHT_DECAY = 0.1
ADAM_EPS = 1e-08
LEARN_RATES = (0.03, 0.1, 0.03, 0.015, 0.2, 0.2)


def layer_norm(values, gain_vec, shift_vec):
    center = values - jnp.mean(values, axis=-1, keepdims=True)
    inverse = lax.rsqrt(jnp.mean(center * center, axis=-1, keepdims=True) + EPSILON)
    normed = center * inverse
    return (normed * gain_vec + shift_vec, normed, inverse)


def norm_back(grad_out, gain_vec, normed, inverse):
    scaled = grad_out * gain_vec
    first_mean = jnp.mean(scaled, axis=-1, keepdims=True)
    second_mean = jnp.mean(scaled * normed, axis=-1, keepdims=True)
    grad_in = inverse * (scaled - first_mean - normed * second_mean)
    return (grad_in, jnp.sum(grad_out * normed, axis=(0, 1)), jnp.sum(grad_out, axis=(0, 1)))


def quick_gelu(values):
    return values * jax.nn.sigmoid(1.702 * values)


def gelu_slope(values):
    sigmoid_vals = jax.nn.sigmoid(1.702 * values)
    return sigmoid_vals + 1.702 * values * sigmoid_vals * (1.0 - sigmoid_vals)


def adam_update(master, moment_one, moment_two, gradient, learn_rate):
    new_first = BETA_FIRST * moment_one + (1.0 - BETA_FIRST) * gradient
    new_second = BETA_SECOND * moment_two + (1.0 - BETA_SECOND) * gradient * gradient
    fixed_first = new_first / (1.0 - BETA_FIRST**STEP)
    fixed_second = new_second / (1.0 - BETA_SECOND**STEP)
    new_master = master - learn_rate * (
        fixed_first / (jnp.sqrt(fixed_second) + ADAM_EPS) + WEIGHT_DECAY * master
    )
    return (new_master, new_first, new_second, new_master.astype(jnp.bfloat16))


def forward(inputs, weights):
    qkv_weight, out_weight, up_weight, down_weight, norm_vec, inner_vec = weights
    images, length, model_width = inputs.shape
    local_width = qkv_weight.shape[2]
    split_heads = (images, length, local_width // HD, HD)
    score_scale = HD ** (-0.5)
    normed_in, hat_in, inv_in = layer_norm(inputs, norm_vec[0], norm_vec[1])
    attn_in = normed_in.astype(jnp.bfloat16)
    project = jnp.einsum("bsd,cde->cbse", attn_in, qkv_weight, preferred_element_type=jnp.float32)
    queries = (project[0] + inner_vec[0]).astype(jnp.bfloat16).reshape(split_heads)
    key_vecs = project[1].astype(jnp.bfloat16).reshape(split_heads)
    values = (project[2] + inner_vec[1]).astype(jnp.bfloat16).reshape(split_heads)
    scores = (
        jnp.einsum("bshe,bthe->bhst", queries, key_vecs, preferred_element_type=jnp.float32)
        * score_scale
    )
    top_score = jnp.max(scores, axis=-1, keepdims=True)
    exp_scores = jnp.exp(scores - top_score)
    row_total = jnp.sum(exp_scores, axis=-1, keepdims=True)
    probs_low = (exp_scores / row_total).astype(jnp.bfloat16)
    mixed_low = jnp.einsum("bhst,bthe->bshe", probs_low, values, preferred_element_type=jnp.float32)
    mixed_low = mixed_low.reshape(images, length, local_width).astype(jnp.bfloat16)
    attn_part = jnp.einsum("bsk,kd->bsd", mixed_low, out_weight, preferred_element_type=jnp.float32)
    attn_out = lax.psum(attn_part.astype(jnp.bfloat16), "tensor").astype(jnp.float32) + norm_vec[4]
    hidden = inputs + attn_out
    normed_mid, hat_mid, inv_mid = layer_norm(hidden, norm_vec[2], norm_vec[3])
    mlp_in = normed_mid.astype(jnp.bfloat16)
    pre_act = jnp.einsum(
        "bsd,dk->bsk", mlp_in, up_weight, preferred_element_type=jnp.float32
    ) + inner_vec[2:].reshape(-1)
    act_vals = quick_gelu(pre_act).astype(jnp.bfloat16)
    mlp_part = jnp.einsum("bsk,kd->bsd", act_vals, down_weight, preferred_element_type=jnp.float32)
    mlp_out = lax.psum(mlp_part.astype(jnp.bfloat16), "tensor").astype(jnp.float32) + norm_vec[5]
    result = hidden + mlp_out
    kept_vals = (
        hat_in,
        inv_in,
        attn_in,
        queries,
        key_vecs,
        values,
        top_score,
        row_total,
        mixed_low,
        hat_mid,
        inv_mid,
        mlp_in,
        pre_act,
        act_vals,
    )
    return (result, kept_vals)


def backward(grad_out, weights, kept_vals):
    qkv_weight, out_weight, up_weight, down_weight, norm_vec, inner_vec = weights
    (
        hat_in,
        inv_in,
        attn_in,
        queries,
        key_vecs,
        values,
        top_score,
        row_total,
        mixed_low,
        hat_mid,
        inv_mid,
        mlp_in,
        pre_act,
        act_vals,
    ) = kept_vals
    images, length, heads_here, head_size = queries.shape
    local_width = heads_here * head_size
    model_width = up_weight.shape[0]
    score_scale = head_size ** (-0.5)
    branch_grad = grad_out.astype(jnp.bfloat16)
    down_grad = jnp.einsum("bsk,bsd->kd", act_vals, branch_grad, preferred_element_type=jnp.float32)
    act_grad = jnp.einsum(
        "bsd,kd->bsk", branch_grad, down_weight, preferred_element_type=jnp.float32
    )
    pre_grad = (act_grad * gelu_slope(pre_act)).astype(jnp.bfloat16)
    up_grad = jnp.einsum("bsd,bsk->dk", mlp_in, pre_grad, preferred_element_type=jnp.float32)
    mid_part = jnp.einsum("bsk,dk->bsd", pre_grad, up_weight, preferred_element_type=jnp.float32)
    mid_grad = lax.psum(mid_part.astype(jnp.bfloat16), "tensor").astype(jnp.float32)
    hidden_add, gain_mid, shift_mid = norm_back(mid_grad, norm_vec[2], hat_mid, inv_mid)
    hidden_grad = grad_out + hidden_add
    attn_grad = hidden_grad.astype(jnp.bfloat16)
    out_grad = jnp.einsum("bsk,bsd->kd", mixed_low, attn_grad, preferred_element_type=jnp.float32)
    mixed_grad = jnp.einsum(
        "bsd,kd->bsk", attn_grad, out_weight, preferred_element_type=jnp.float32
    )
    mixed_grad = mixed_grad.astype(jnp.bfloat16).reshape(queries.shape)
    scores = (
        jnp.einsum("bshe,bthe->bhst", queries, key_vecs, preferred_element_type=jnp.float32)
        * score_scale
    )
    probs_full = jnp.exp(scores - top_score) / row_total
    probs_low = probs_full.astype(jnp.bfloat16)
    value_grad = jnp.einsum(
        "bhst,bshe->bthe", probs_low, mixed_grad, preferred_element_type=jnp.float32
    ).astype(jnp.bfloat16)
    prob_grad = jnp.einsum(
        "bshe,bthe->bhst", mixed_grad, values, preferred_element_type=jnp.float32
    )
    score_grad = (
        probs_full * (prob_grad - jnp.sum(probs_full * prob_grad, axis=-1, keepdims=True))
    ).astype(jnp.bfloat16)
    query_grad = (
        jnp.einsum("bhst,bthe->bshe", score_grad, key_vecs, preferred_element_type=jnp.float32)
        * score_scale
    ).astype(jnp.bfloat16)
    key_grad = (
        jnp.einsum("bhst,bshe->bthe", score_grad, queries, preferred_element_type=jnp.float32)
        * score_scale
    ).astype(jnp.bfloat16)
    stacked = jnp.stack([query_grad, key_grad, value_grad]).reshape(3, images, length, local_width)
    qkv_grad = jnp.einsum("bsd,cbse->cde", attn_in, stacked, preferred_element_type=jnp.float32)
    in_part = jnp.einsum("cbse,cde->bsd", stacked, qkv_weight, preferred_element_type=jnp.float32)
    in_grad = lax.psum(in_part.astype(jnp.bfloat16), "tensor").astype(jnp.float32)
    input_add, gain_in, shift_in = norm_back(in_grad, norm_vec[0], hat_in, inv_in)
    input_grad = hidden_grad + input_add
    stacked_sums = jnp.sum(stacked, axis=(1, 2), dtype=jnp.float32)
    norm_grad = jnp.stack(
        [
            gain_in,
            shift_in,
            gain_mid,
            shift_mid,
            jnp.sum(attn_grad, axis=(0, 1), dtype=jnp.float32),
            jnp.sum(branch_grad, axis=(0, 1), dtype=jnp.float32),
        ]
    )
    unit_sums = jnp.sum(pre_grad, axis=(0, 1), dtype=jnp.float32).reshape(-1, local_width)
    inner_grad = jnp.concatenate([stacked_sums[0:1], stacked_sums[2:3], unit_sums], axis=0)
    up_shaped = up_grad.reshape(model_width, -1, local_width)
    down_shaped = down_grad.reshape(-1, local_width, model_width)
    return (input_grad, (qkv_grad, out_grad, up_shaped, down_shaped, norm_grad, inner_grad))


def on_device(
    inputs,
    cotangent,
    image_flags,
    qkv_master,
    qkv_first,
    qkv_second,
    out_master,
    out_first,
    out_second,
    up_master,
    up_first,
    up_second,
    down_master,
    down_first,
    down_second,
    norm_master,
    norm_first,
    norm_second,
    inner_master,
    inner_first,
    inner_second,
):
    gathered = (
        lax.all_gather(qkv_master.astype(jnp.bfloat16), "dp", axis=1, tiled=True),
        lax.all_gather(out_master.astype(jnp.bfloat16), "dp", axis=0, tiled=True),
        lax.all_gather(up_master.astype(jnp.bfloat16), "dp", axis=0, tiled=True),
        lax.all_gather(down_master.astype(jnp.bfloat16), "dp", axis=1, tiled=True),
        lax.all_gather(norm_master.astype(jnp.bfloat16), "dp", axis=1, tiled=True),
        lax.all_gather(inner_master.astype(jnp.bfloat16), "dp", axis=1, tiled=True),
    )
    qkv_weight, out_weight, up_whole, down_whole, norm_low, inner_low = gathered
    model_width = qkv_weight.shape[1]
    weights = (
        qkv_weight,
        out_weight,
        up_whole.reshape(model_width, -1),
        down_whole.reshape(-1, model_width),
        norm_low.astype(jnp.float32),
        inner_low.astype(jnp.float32),
    )
    inputs_wide = inputs.astype(jnp.float32)
    result, kept_vals = forward(inputs_wide, weights)
    grad_out = cotangent.astype(jnp.float32) * image_flags.astype(jnp.float32)[:, None, None]
    input_grad, local_grads = backward(grad_out, weights, kept_vals)
    shares = tuple(
        lax.psum_scatter(
            full_grad.astype(jnp.bfloat16), "dp", scatter_dimension=along_dim, tiled=True
        ).astype(jnp.float32)
        for full_grad, along_dim in zip(local_grads, (1, 0, 0, 1, 1, 1))
    )
    qkv_new = adam_update(qkv_master, qkv_first, qkv_second, shares[0], LEARN_RATES[0])
    out_new = adam_update(out_master, out_first, out_second, shares[1], LEARN_RATES[1])
    up_new = adam_update(up_master, up_first, up_second, shares[2], LEARN_RATES[2])
    down_new = adam_update(down_master, down_first, down_second, shares[3], LEARN_RATES[3])
    norm_new = adam_update(norm_master, norm_first, norm_second, shares[4], LEARN_RATES[4])
    inner_new = adam_update(inner_master, inner_first, inner_second, shares[5], LEARN_RATES[5])
    return (
        result.astype(jnp.bfloat16),
        input_grad,
        qkv_new[0],
        qkv_new[1],
        qkv_new[2],
        qkv_new[3],
        out_new[0],
        out_new[1],
        out_new[2],
        out_new[3],
        up_new[0],
        up_new[1],
        up_new[2],
        up_new[3],
        down_new[0],
        down_new[1],
        down_new[2],
        down_new[3],
        norm_new[0],
        norm_new[1],
        norm_new[2],
        norm_new[3],
        inner_new[0],
        inner_new[1],
        inner_new[2],
        inner_new[3],
    )


def solution(mesh):
    placed = (
        P("dp", None, None),
        P("dp", None, None),
        P("dp"),
        P(None, "dp", "tensor"),
        P(None, "dp", "tensor"),
        P(None, "dp", "tensor"),
        P(("tensor", "dp"), None),
        P(("tensor", "dp"), None),
        P(("tensor", "dp"), None),
        P("dp", None, "tensor"),
        P("dp", None, "tensor"),
        P("dp", None, "tensor"),
        P(None, ("tensor", "dp"), None),
        P(None, ("tensor", "dp"), None),
        P(None, ("tensor", "dp"), None),
        P(None, "dp"),
        P(None, "dp"),
        P(None, "dp"),
        P(None, ("tensor", "dp")),
        P(None, ("tensor", "dp")),
        P(None, ("tensor", "dp")),
    )
    return jax.shard_map(
        on_device,
        mesh=mesh,
        in_specs=placed,
        out_specs=(
            P("dp", None, None),
            P("dp", None, None),
            P(None, "dp", "tensor"),
            P(None, "dp", "tensor"),
            P(None, "dp", "tensor"),
            P(None, "dp", "tensor"),
            P(("tensor", "dp"), None),
            P(("tensor", "dp"), None),
            P(("tensor", "dp"), None),
            P(("tensor", "dp"), None),
            P("dp", None, "tensor"),
            P("dp", None, "tensor"),
            P("dp", None, "tensor"),
            P("dp", None, "tensor"),
            P(None, ("tensor", "dp"), None),
            P(None, ("tensor", "dp"), None),
            P(None, ("tensor", "dp"), None),
            P(None, ("tensor", "dp"), None),
            P(None, "dp"),
            P(None, "dp"),
            P(None, "dp"),
            P(None, "dp"),
            P(None, ("tensor", "dp")),
            P(None, ("tensor", "dp")),
            P(None, ("tensor", "dp")),
            P(None, ("tensor", "dp")),
        ),
        check_vma=False,
    )
```

```python
import math

import jax
import jax.numpy as jnp
from jax import lax
from jax.experimental import pallas as pl
from jax.experimental.pallas import tpu as pltpu
from jax.sharding import PartitionSpec as P

HD = 64
STEP = 5


EPSILON = 1e-05
BETA_FIRST = 0.5
BETA_SECOND = 0.5
WEIGHT_DECAY = 0.1
ADAM_EPS = 1e-08
LEARN_RATES = (0.03, 0.1, 0.03, 0.015, 0.2, 0.2)


def layer_norm(values, gain_vec, shift_vec):
    center = values - jnp.mean(values, axis=-1, keepdims=True)
    inverse = lax.rsqrt(jnp.mean(center * center, axis=-1, keepdims=True) + EPSILON)
    normed = center * inverse
    return (normed * gain_vec + shift_vec, normed, inverse)


def norm_back(grad_out, gain_vec, normed, inverse):
    scaled = grad_out * gain_vec
    first_mean = jnp.mean(scaled, axis=-1, keepdims=True)
    second_mean = jnp.mean(scaled * normed, axis=-1, keepdims=True)
    grad_in = inverse * (scaled - first_mean - normed * second_mean)
    return (grad_in, jnp.sum(grad_out * normed, axis=(0, 1)), jnp.sum(grad_out, axis=(0, 1)))


def quick_gelu(values):
    return values * jax.nn.sigmoid(1.702 * values)


def gelu_slope(values):
    sigmoid_vals = jax.nn.sigmoid(1.702 * values)
    return sigmoid_vals + 1.702 * values * sigmoid_vals * (1.0 - sigmoid_vals)


def adam_update(master, moment_one, moment_two, gradient, learn_rate):
    new_first = BETA_FIRST * moment_one + (1.0 - BETA_FIRST) * gradient
    new_second = BETA_SECOND * moment_two + (1.0 - BETA_SECOND) * gradient * gradient
    fixed_first = new_first / (1.0 - BETA_FIRST**STEP)
    fixed_second = new_second / (1.0 - BETA_SECOND**STEP)
    new_master = master - learn_rate * (
        fixed_first / (jnp.sqrt(fixed_second) + ADAM_EPS) + WEIGHT_DECAY * master
    )
    return (new_master, new_first, new_second, new_master.astype(jnp.bfloat16))


def forward(inputs, weights):
    qkv_weight, out_weight, up_weight, down_weight, norm_vec, inner_vec = weights
    images, length, model_width = inputs.shape
    local_width = qkv_weight.shape[2]
    split_heads = (images, length, local_width // HD, HD)
    score_scale = HD ** (-0.5)
    normed_in, hat_in, inv_in = layer_norm(inputs, norm_vec[0], norm_vec[1])
    attn_in = normed_in.astype(jnp.bfloat16)
    project = jnp.einsum("bsd,cde->cbse", attn_in, qkv_weight, preferred_element_type=jnp.float32)
    queries = (project[0] + inner_vec[0]).astype(jnp.bfloat16).reshape(split_heads)
    key_vecs = project[1].astype(jnp.bfloat16).reshape(split_heads)
    values = (project[2] + inner_vec[1]).astype(jnp.bfloat16).reshape(split_heads)
    scores = (
        jnp.einsum("bshe,bthe->bhst", queries, key_vecs, preferred_element_type=jnp.float32)
        * score_scale
    )
    top_score = jnp.max(scores, axis=-1, keepdims=True)
    exp_scores = jnp.exp(scores - top_score)
    row_total = jnp.sum(exp_scores, axis=-1, keepdims=True)
    probs_low = (exp_scores / row_total).astype(jnp.bfloat16)
    mixed_low = jnp.einsum("bhst,bthe->bshe", probs_low, values, preferred_element_type=jnp.float32)
    mixed_low = mixed_low.reshape(images, length, local_width).astype(jnp.bfloat16)
    attn_part = jnp.einsum("bsk,kd->bsd", mixed_low, out_weight, preferred_element_type=jnp.float32)
    attn_out = lax.psum(attn_part.astype(jnp.bfloat16), "tensor").astype(jnp.float32) + norm_vec[4]
    hidden = inputs + attn_out
    normed_mid, hat_mid, inv_mid = layer_norm(hidden, norm_vec[2], norm_vec[3])
    mlp_in = normed_mid.astype(jnp.bfloat16)
    pre_act = jnp.einsum(
        "bsd,dk->bsk", mlp_in, up_weight, preferred_element_type=jnp.float32
    ) + inner_vec[2:].reshape(-1)
    act_vals = quick_gelu(pre_act).astype(jnp.bfloat16)
    mlp_part = jnp.einsum("bsk,kd->bsd", act_vals, down_weight, preferred_element_type=jnp.float32)
    mlp_out = lax.psum(mlp_part.astype(jnp.bfloat16), "tensor").astype(jnp.float32) + norm_vec[5]
    result = hidden + mlp_out
    kept_vals = (
        hat_in,
        inv_in,
        attn_in,
        queries,
        key_vecs,
        values,
        top_score,
        row_total,
        mixed_low,
        hat_mid,
        inv_mid,
        mlp_in,
        pre_act,
        act_vals,
    )
    return (result, kept_vals)


def backward(grad_out, weights, kept_vals):
    qkv_weight, out_weight, up_weight, down_weight, norm_vec, inner_vec = weights
    (
        hat_in,
        inv_in,
        attn_in,
        queries,
        key_vecs,
        values,
        top_score,
        row_total,
        mixed_low,
        hat_mid,
        inv_mid,
        mlp_in,
        pre_act,
        act_vals,
    ) = kept_vals
    images, length, heads_here, head_size = queries.shape
    local_width = heads_here * head_size
    model_width = up_weight.shape[0]
    score_scale = head_size ** (-0.5)
    branch_grad = grad_out.astype(jnp.bfloat16)
    down_grad = jnp.einsum("bsk,bsd->kd", act_vals, branch_grad, preferred_element_type=jnp.float32)
    act_grad = jnp.einsum(
        "bsd,kd->bsk", branch_grad, down_weight, preferred_element_type=jnp.float32
    )
    pre_grad = (act_grad * gelu_slope(pre_act)).astype(jnp.bfloat16)
    up_grad = jnp.einsum("bsd,bsk->dk", mlp_in, pre_grad, preferred_element_type=jnp.float32)
    mid_part = jnp.einsum("bsk,dk->bsd", pre_grad, up_weight, preferred_element_type=jnp.float32)
    mid_grad = lax.psum(mid_part.astype(jnp.bfloat16), "tensor").astype(jnp.float32)
    hidden_add, gain_mid, shift_mid = norm_back(mid_grad, norm_vec[2], hat_mid, inv_mid)
    hidden_grad = grad_out + hidden_add
    attn_grad = hidden_grad.astype(jnp.bfloat16)
    out_grad = jnp.einsum("bsk,bsd->kd", mixed_low, attn_grad, preferred_element_type=jnp.float32)
    mixed_grad = jnp.einsum(
        "bsd,kd->bsk", attn_grad, out_weight, preferred_element_type=jnp.float32
    )
    mixed_grad = mixed_grad.astype(jnp.bfloat16).reshape(queries.shape)
    scores = (
        jnp.einsum("bshe,bthe->bhst", queries, key_vecs, preferred_element_type=jnp.float32)
        * score_scale
    )
    probs_full = jnp.exp(scores - top_score) / row_total
    probs_low = probs_full.astype(jnp.bfloat16)
    value_grad = jnp.einsum(
        "bhst,bshe->bthe", probs_low, mixed_grad, preferred_element_type=jnp.float32
    ).astype(jnp.bfloat16)
    prob_grad = jnp.einsum(
        "bshe,bthe->bhst", mixed_grad, values, preferred_element_type=jnp.float32
    )
    score_grad = (
        probs_full * (prob_grad - jnp.sum(probs_full * prob_grad, axis=-1, keepdims=True))
    ).astype(jnp.bfloat16)
    query_grad = (
        jnp.einsum("bhst,bthe->bshe", score_grad, key_vecs, preferred_element_type=jnp.float32)
        * score_scale
    ).astype(jnp.bfloat16)
    key_grad = (
        jnp.einsum("bhst,bshe->bthe", score_grad, queries, preferred_element_type=jnp.float32)
        * score_scale
    ).astype(jnp.bfloat16)
    stacked = jnp.stack([query_grad, key_grad, value_grad]).reshape(3, images, length, local_width)
    qkv_grad = jnp.einsum("bsd,cbse->cde", attn_in, stacked, preferred_element_type=jnp.float32)
    in_part = jnp.einsum("cbse,cde->bsd", stacked, qkv_weight, preferred_element_type=jnp.float32)
    in_grad = lax.psum(in_part.astype(jnp.bfloat16), "tensor").astype(jnp.float32)
    input_add, gain_in, shift_in = norm_back(in_grad, norm_vec[0], hat_in, inv_in)
    input_grad = hidden_grad + input_add
    stacked_sums = jnp.sum(stacked, axis=(1, 2), dtype=jnp.float32)
    norm_grad = jnp.stack(
        [
            gain_in,
            shift_in,
            gain_mid,
            shift_mid,
            jnp.sum(attn_grad, axis=(0, 1), dtype=jnp.float32),
            jnp.sum(branch_grad, axis=(0, 1), dtype=jnp.float32),
        ]
    )
    unit_sums = jnp.sum(pre_grad, axis=(0, 1), dtype=jnp.float32).reshape(-1, local_width)
    inner_grad = jnp.concatenate([stacked_sums[0:1], stacked_sums[2:3], unit_sums], axis=0)
    up_shaped = up_grad.reshape(model_width, -1, local_width)
    down_shaped = down_grad.reshape(-1, local_width, model_width)
    return (input_grad, (qkv_grad, out_grad, up_shaped, down_shaped, norm_grad, inner_grad))


def on_device(
    inputs,
    cotangent,
    image_flags,
    qkv_master,
    qkv_first,
    qkv_second,
    out_master,
    out_first,
    out_second,
    up_master,
    up_first,
    up_second,
    down_master,
    down_first,
    down_second,
    norm_master,
    norm_first,
    norm_second,
    inner_master,
    inner_first,
    inner_second,
):
    gathered = (
        lax.all_gather(qkv_master.astype(jnp.bfloat16), "dp", axis=1, tiled=True),
        lax.all_gather(out_master.astype(jnp.bfloat16), "dp", axis=0, tiled=True),
        lax.all_gather(up_master.astype(jnp.bfloat16), "dp", axis=0, tiled=True),
        lax.all_gather(down_master.astype(jnp.bfloat16), "dp", axis=1, tiled=True),
        lax.all_gather(norm_master.astype(jnp.bfloat16), "dp", axis=1, tiled=True),
        lax.all_gather(inner_master.astype(jnp.bfloat16), "dp", axis=1, tiled=True),
    )
    qkv_weight, out_weight, up_whole, down_whole, norm_low, inner_low = gathered
    model_width = qkv_weight.shape[1]
    weights = (
        qkv_weight,
        out_weight,
        up_whole.reshape(model_width, -1),
        down_whole.reshape(-1, model_width),
        norm_low.astype(jnp.float32),
        inner_low.astype(jnp.float32),
    )
    inputs_wide = inputs.astype(jnp.float32)
    result, kept_vals = forward(inputs_wide, weights)
    grad_out = cotangent.astype(jnp.float32) * image_flags.astype(jnp.float32)[:, None, None]
    input_grad, local_grads = backward(grad_out, weights, kept_vals)
    shares = tuple(
        lax.psum_scatter(
            full_grad.astype(jnp.bfloat16), "dp", scatter_dimension=along_dim, tiled=True
        ).astype(jnp.float32)
        for full_grad, along_dim in zip(local_grads, (1, 0, 0, 1, 1, 1))
    )
    qkv_new = adam_update(qkv_master, qkv_first, qkv_second, shares[0], LEARN_RATES[0])
    out_new = adam_update(out_master, out_first, out_second, shares[1], LEARN_RATES[1])
    up_new = adam_update(up_master, up_first, up_second, shares[2], LEARN_RATES[2])
    down_new = adam_update(down_master, down_first, down_second, shares[3], LEARN_RATES[3])
    norm_new = adam_update(norm_master, norm_first, norm_second, shares[4], LEARN_RATES[4])
    inner_new = adam_update(inner_master, inner_first, inner_second, shares[5], LEARN_RATES[5])
    return (
        result.astype(jnp.bfloat16),
        input_grad,
        qkv_new[0],
        qkv_new[1],
        qkv_new[2],
        qkv_new[3],
        out_new[0],
        out_new[1],
        out_new[2],
        out_new[3],
        up_new[0],
        up_new[1],
        up_new[2],
        up_new[3],
        down_new[0],
        down_new[1],
        down_new[2],
        down_new[3],
        norm_new[0],
        norm_new[1],
        norm_new[2],
        norm_new[3],
        inner_new[0],
        inner_new[1],
        inner_new[2],
        inner_new[3],
    )


def partner_swap(values, bit_name):
    if bit_name == "x":
        return lax.ppermute(values, "tensor", [(0, 1), (1, 0)])
    mask = {"c": 1, "y": 2, "l": 4, "h": 8}[bit_name]
    size = lax.axis_size("dp")
    return lax.ppermute(values, "dp", [(index, index ^ mask) for index in range(size)])


def bits_here():
    place = lax.axis_index("dp")
    return {
        "x": lax.axis_index("tensor"),
        "c": place & 1,
        "y": (place >> 1) & 1,
        "l": (place >> 2) & 1,
        "h": (place >> 3) & 1,
    }


def joined(mine, other, bit, axis):
    lower = jnp.where(bit == 0, mine, other)
    upper = jnp.where(bit == 0, other, mine)
    return jnp.concatenate([lower, upper], axis=axis)


def gather_tree(piece, stages, bits):
    for name, axis in stages:
        piece = joined(piece, partner_swap(piece, name), bits[name], axis)
    return piece


def halves_at(values, bit, axis):
    half = values.shape[axis] // 2
    keep = lax.dynamic_slice_in_dim(values, bit * half, half, axis)
    give = lax.dynamic_slice_in_dim(values, (1 - bit) * half, half, axis)
    return keep, give


def scatter_tree(whole, stages, bits):
    for name, axis in stages:
        keep, give = halves_at(whole, bits[name], axis)
        whole = (
            keep.astype(jnp.float32) + partner_swap(give, name).astype(jnp.float32)
        ).astype(jnp.bfloat16)
    return whole


def tie(values):
    return lax.optimization_barrier(values)


def to_pair(values):
    size = lax.axis_size("dp")
    pairs = [(2 * at, 2 * (at + 1)) for at in range(0, size, 2)]
    pairs += [(2 * (at + 1) + 1, 2 * at + 1) for at in range(0, size, 2)]
    return lax.ppermute(values, ("dp", "tensor"), pairs)


def to_owner(values):
    size = lax.axis_size("dp")
    pairs = [(2 * at, 2 * at + 1) for at in range(0, size, 2)]
    pairs += [(2 * (at + 1) + 1, 2 * (at + 1)) for at in range(0, size, 2)]
    return lax.ppermute(values, ("dp", "tensor"), pairs)


def dot_in(left_side, right_side, left_dim, right_dim):
    return lax.dot_general(
        left_side,
        right_side,
        (((left_dim,), (right_dim,)), ((), ())),
        preferred_element_type=jnp.float32,
    )


def attend_body(query_ref, key_ref, value_ref, mixed_ref, level_ref):
    scale = HD**-0.5 * math.log2(math.e)
    parts = []
    for head in range(2):
        cols = slice(head * HD, (head + 1) * HD)
        query, key, value = query_ref[0, :, cols], key_ref[0, :, cols], value_ref[0, :, cols]
        scores = dot_in(key, query, 1, 1)
        top = jnp.max(scores, axis=0, keepdims=True) * scale
        powers = jnp.exp2(scores * scale - top)
        total = jnp.sum(powers, axis=0, keepdims=True)
        parts.append(dot_in(value, powers.astype(jnp.bfloat16), 0, 0) * (1.0 / total))
        level_ref[0, 0, head : head + 1] = top + jnp.log2(total)
    mixed_ref[0] = jnp.concatenate(parts, 0).T.astype(jnp.bfloat16)


def attend(queries, key_vecs, values):
    images, length, width = queries.shape
    pairs = width // (2 * HD)
    cols = pl.BlockSpec((1, length, 2 * HD), lambda image, pair: (image, 0, pair))
    level = pl.BlockSpec((1, 1, 2, length), lambda image, pair: (image, pair, 0, 0))
    work = images * pairs * 2 * length * length
    return pl.pallas_call(
        attend_body,
        grid=(images, pairs),
        in_specs=[cols, cols, cols],
        out_specs=[cols, level],
        out_shape=[
            jax.ShapeDtypeStruct(queries.shape, jnp.bfloat16),
            jax.ShapeDtypeStruct((images, pairs, 2, length), jnp.float32),
        ],
        compiler_params=pltpu.CompilerParams(vmem_limit_bytes=40 * 2**20),
        cost_estimate=pl.CostEstimate(
            flops=work * HD * 16, bytes_accessed=queries.size * 8, transcendentals=work
        ),
    )(queries, key_vecs, values)


def attend_back_body(query_ref, key_ref, value_ref, grad_ref, level_ref, dq_ref, dk_ref, dv_ref):
    scale = HD**-0.5 * math.log2(math.e)
    dq_parts, dk_parts, dv_parts = [], [], []
    for head in range(2):
        cols = slice(head * HD, (head + 1) * HD)
        query, key, value = query_ref[0, :, cols], key_ref[0, :, cols], value_ref[0, :, cols]
        grad = grad_ref[0, :, cols]
        probs = jnp.exp2(dot_in(key, query, 1, 1) * scale - level_ref[0, 0, head : head + 1])
        prob_grad = dot_in(value, grad, 1, 1)
        dv_parts.append(dot_in(probs.astype(jnp.bfloat16), grad, 1, 0))
        row_sum = jnp.sum(probs * prob_grad, axis=0, keepdims=True)
        score_grad = (probs * (prob_grad - row_sum)).astype(jnp.bfloat16)
        dq_parts.append(dot_in(key, score_grad, 0, 0) * HD**-0.5)
        dk_parts.append(dot_in(score_grad, query, 1, 0) * HD**-0.5)
    dq_ref[0] = jnp.concatenate(dq_parts, 0).T.astype(jnp.bfloat16)
    dk_ref[0] = jnp.concatenate(dk_parts, 1).astype(jnp.bfloat16)
    dv_ref[0] = jnp.concatenate(dv_parts, 1).astype(jnp.bfloat16)


def attend_back(queries, key_vecs, values, mixed_grad, level, part, parts):
    images, length, width = queries.shape
    pairs = width // (2 * HD)
    here = pairs // parts
    cols = pl.BlockSpec((1, length, 2 * HD), lambda image, at: (image, 0, at * parts + part))
    levels = pl.BlockSpec((1, 1, 2, length), lambda image, at: (image, at * parts + part, 0, 0))
    outs = pl.BlockSpec((1, length, 2 * HD), lambda image, at: (image, 0, at))
    work = images * here * 2 * length * length
    shape = jax.ShapeDtypeStruct((images, length, width // parts), jnp.bfloat16)
    return pl.pallas_call(
        attend_back_body,
        grid=(images, here),
        in_specs=[cols, cols, cols, cols, levels],
        out_specs=[outs] * 3,
        out_shape=[shape] * 3,
        compiler_params=pltpu.CompilerParams(vmem_limit_bytes=40 * 2**20),
        cost_estimate=pl.CostEstimate(
            flops=work * HD * 40, bytes_accessed=queries.size * 14 // parts, transcendentals=work
        ),
    )(queries, key_vecs, values, mixed_grad, level)


ROWS = 296


def row_calls(body, arrays, vectors, outs, sums):
    images, length, width = arrays[0].shape
    steps = pl.cdiv(length, ROWS)
    block = pl.BlockSpec((1, ROWS, width), lambda image, step: (image, step, 0))
    once = lambda image, step: (0, 0)
    total = sum(one.size * one.dtype.itemsize for one in arrays)
    total += sum(arrays[0].size * jnp.dtype(kind).itemsize for kind in outs)

    def kernel(*refs):
        taken = refs[: len(arrays)]
        given = refs[len(arrays) : len(arrays) + len(vectors)]
        made = refs[len(arrays) + len(vectors) :][: len(outs)]
        row_at = pl.program_id(1) * ROWS + lax.broadcasted_iota(jnp.int32, (ROWS, 1), 0)
        inside = row_at < length
        results, added = body(
            [jnp.where(inside, ref[0].astype(jnp.float32), 0.0) for ref in taken],
            [ref[...] for ref in given],
        )
        for ref, value in zip(made, results):
            ref[0] = value.astype(ref.dtype)
        if sums:
            first = jnp.logical_and(pl.program_id(0) == 0, pl.program_id(1) == 0)
            sum_ref = refs[-1]

            @pl.when(first)
            def _():
                sum_ref[...] = jnp.zeros_like(sum_ref)

            rows = [jnp.sum(jnp.where(inside, value, 0.0), axis=0, keepdims=True) for value in added]
            sum_ref[...] += jnp.concatenate(rows, 0)

    return pl.pallas_call(
        kernel,
        grid=(images, steps),
        in_specs=[block] * len(arrays) + [pl.BlockSpec(one.shape, once) for one in vectors],
        out_specs=[block] * len(outs) + ([pl.BlockSpec((sums, width), once)] if sums else []),
        out_shape=[jax.ShapeDtypeStruct(arrays[0].shape, kind) for kind in outs]
        + ([jax.ShapeDtypeStruct((sums, width), jnp.float32)] if sums else []),
        compiler_params=pltpu.CompilerParams(vmem_limit_bytes=48 * 2**20),
        cost_estimate=pl.CostEstimate(
            flops=20 * arrays[0].size, bytes_accessed=total, transcendentals=0
        ),
    )(*arrays, *vectors)


def normed_of(values):
    center = values - jnp.mean(values, axis=-1, keepdims=True)
    inverse = lax.rsqrt(jnp.mean(center * center, axis=-1, keepdims=True) + EPSILON)
    return center * inverse, inverse


def pick_body(arrays, vectors):
    home = vectors[0][0:1, 0:1]
    return [arrays[0] * home + arrays[1] * (1.0 - home)], []


def first_norm_body(arrays, vectors):
    normed, _ = normed_of(arrays[0])
    return [normed * vectors[0][0:1] + vectors[0][1:2]], []


def second_norm_body(arrays, vectors):
    hidden = arrays[0] + (arrays[1] + arrays[2] + vectors[0][4:5])
    normed, _ = normed_of(hidden)
    return [hidden, normed * vectors[0][2:3] + vectors[0][3:4]], []


def norm_back_body(gain_row, with_total):
    def body(arrays, vectors):
        mine, other, values, above = arrays
        grad = mine + other
        normed, inverse = normed_of(values)
        scaled = grad * vectors[0][gain_row : gain_row + 1]
        first_mean = jnp.mean(scaled, axis=-1, keepdims=True)
        second_mean = jnp.mean(scaled * normed, axis=-1, keepdims=True)
        result = above + inverse * (scaled - first_mean - normed * second_mean)
        result = result.astype(jnp.bfloat16).astype(jnp.float32)
        added = [grad * normed, grad] + ([result] if with_total else [])
        return [result], added

    return body


def on_chip_pair(
    inputs,
    cotangent,
    image_flags,
    qkv_master,
    qkv_first,
    qkv_second,
    out_master,
    out_first,
    out_second,
    up_master,
    up_first,
    up_second,
    down_master,
    down_first,
    down_second,
    norm_master,
    norm_first,
    norm_second,
    inner_master,
    inner_first,
    inner_second,
):
    bits = bits_here()
    core, tens = bits["c"], bits["x"]
    at_home = core == tens
    low = jnp.bfloat16
    model_width = inputs.shape[2]
    rows_here = qkv_master.shape[1]
    width = qkv_master.shape[2]
    half_width = width // 2
    unit_rows = up_master.shape[1]
    out_rows = out_master.shape[0]

    small = jnp.concatenate([norm_master.astype(low), inner_master.astype(low)], axis=1)
    small = gather_tree(
        small[None, None, None, None, None], [("c", 4), ("h", 1), ("l", 2), ("y", 3), ("x", 0)], bits
    )
    small = small.reshape(2, -1, 6, rows_here + out_rows).astype(jnp.float32)
    norm_vec = small[0, :, :, :rows_here].transpose(1, 0, 2).reshape(6, model_width)
    inner_all = small[:, :, :, rows_here:].transpose(2, 0, 1, 3).reshape(6, 2, width)

    f32 = jnp.float32

    qkv_low = qkv_master.astype(low).reshape(3, rows_here, 2, half_width)
    keep, give = halves_at(qkv_low, core, 2)
    other = partner_swap(give, "c")
    qkv_piece = joined(keep[:, :, 0], other[:, :, 0], core, 1)[:, None, None, None]
    out_low = out_master.astype(low)
    out_pair = joined(out_low, partner_swap(out_low, "c"), core, 0)
    keep, give = halves_at(up_master.astype(low), core, 1)
    other = partner_swap(give, "c")
    up_piece = joined(keep, other, core, 0).transpose(1, 0, 2)[:, None, None, None]
    keep, give = halves_at(down_master.astype(low), core, 0)
    other = partner_swap(give, "c")
    down_piece = joined(keep, other, core, 1)[:, None, None, None, None]
    tree_a = ("h", "l", "x", "y")
    tree_b = ("h", "l", "y", "x")
    qkv_axes = {"h": 1, "l": 2, "y": 3, "x": -1}
    out_axes = {"x": 0, "l": 1, "y": 2}
    up_axes = {"h": 0, "l": 1, "y": 2, "x": -1}
    down_axes = {"x": 0, "h": 1, "l": 2, "y": 3}

    def swap_all(pieces, names):
        return [partner_swap(piece, name) for piece, name in zip(pieces, names)]

    def join_all(pieces, others, names, axes):
        return [
            joined(piece, other, bits[name], axis[name])
            for piece, other, name, axis in zip(pieces, others, names, axes)
        ]

    flag_vals = image_flags.astype(f32)[:, None, None]
    flagged = (cotangent.astype(f32) * flag_vals).astype(low)
    tokens = jnp.where(at_home, inputs, to_pair(inputs))
    branch_grad = jnp.where(at_home, flagged, to_pair(flagged))

    qkv = [qkv_piece[:2], qkv_piece[2:]]
    two = [qkv_axes, qkv_axes]
    for name in ("h", "l"):
        qkv = join_all(qkv, swap_all(qkv, (name, name)), (name, name), two)
    (attn_in,) = row_calls(first_norm_body, [tokens], [norm_vec], [low], 0)
    up = [up_piece[0], up_piece[1]]
    down = [down_piece[0], down_piece[1]]
    ups, downs = [up_axes, up_axes], [down_axes, down_axes]
    qkv, up, out_pair = tie((qkv, up, out_pair))
    got, got_up = swap_all(qkv, ("x", "y")), swap_all(up, ("h", "h"))
    got, got_up = tie((got, got_up))
    qkv = join_all(qkv, got, ("x", "y"), two)
    up = join_all(up, got_up, ("h", "h"), ups)
    got, got_up = swap_all(qkv, ("y", "x")), swap_all(up, ("l", "l"))
    out_other = partner_swap(out_pair, "h")
    got, got_up, out_other, attn_in, branch_grad, down = tie(
        (got, got_up, out_other, attn_in, branch_grad, down)
    )
    qkv = join_all(qkv, got, ("y", "x"), two)
    up = join_all(up, got_up, ("l", "l"), ups)
    qk_weight = qkv[0].reshape(2, model_width, width)
    v_weight = qkv[1].reshape(model_width, width)
    out = [jnp.where(bits["h"] == core, out_pair, out_other)[None, None, None]]

    images, length, _ = tokens.shape
    head_bias = lax.dynamic_slice_in_dim(inner_all[:2], core * half_width, half_width, 2).reshape(2, width)
    unit_bias = lax.dynamic_slice_in_dim(inner_all[2:], core * 2, 2, 0).reshape(2, -1)

    def project(form, left_side, right_side):
        return jnp.einsum(form, left_side, right_side, preferred_element_type=f32)

    got_up, got_out, got_down = swap_all(up, ("x", "y")), swap_all(out, "l"), swap_all(down, ("h", "h"))
    queries = (project("bsd,de->bse", attn_in, qk_weight[0]) + head_bias[0]).astype(low)
    key_vecs = project("bsd,de->bse", attn_in, qk_weight[1]).astype(low)
    values = (project("bsd,de->bse", attn_in, v_weight) + head_bias[1]).astype(low)
    got_up, got_out, got_down, queries, key_vecs, values = tie(
        (got_up, got_out, got_down, queries, key_vecs, values)
    )
    up = join_all(up, got_up, ("x", "y"), ups)
    out = join_all(out, got_out, "l", [out_axes])
    down = join_all(down, got_down, ("h", "h"), downs)

    got_out = swap_all(out, "y")
    got_up = swap_all(up, ("y", "x"))
    got_down = swap_all(down, ("l", "l"))
    mixed_low, level = attend(queries, key_vecs, values)
    got_up, got_out, got_down, mixed_low, level = tie((got_up, got_out, got_down, mixed_low, level))
    out = join_all(out, got_out, "y", [out_axes])
    (out_weight,) = join_all(out, swap_all(out, "x"), "x", [out_axes])
    out_weight = out_weight.reshape(width, model_width)
    up = join_all(up, got_up, ("y", "x"), ups)
    up_weights = [piece.reshape(model_width, -1) for piece in up]
    down = join_all(down, got_down, ("l", "l"), downs)

    got_down = swap_all(down, ("x", "y"))
    attn_part = project("bsk,kd->bsd", mixed_low, out_weight).astype(low)
    got_down, attn_part = tie((got_down, attn_part))
    down = join_all(down, got_down, ("x", "y"), downs)
    got_down = swap_all(down, ("y", "x"))
    hidden, mlp_in = row_calls(
        second_norm_body, [tokens, attn_part, partner_swap(attn_part, "c")], [norm_vec], [f32, low], 0
    )

    act_vals, slopes = [], []
    for at in range(2):
        pre_act = project("bsd,dk->bsk", mlp_in, up_weights[at]) + unit_bias[at]
        sigmoid_vals = jax.nn.sigmoid(1.702 * pre_act)
        act_vals.append((pre_act * sigmoid_vals).astype(low))
        slopes.append((sigmoid_vals + 1.702 * pre_act * sigmoid_vals * (1.0 - sigmoid_vals)).astype(low))
    act_vals, slopes = tie((act_vals, slopes))
    down_grads = [project("bsk,bsd->kd", act, branch_grad).astype(low) for act in act_vals]
    down_grads, got_down, act_vals, branch_grad = tie((down_grads, got_down, act_vals, branch_grad))
    down = join_all(down, got_down, ("y", "x"), downs)
    down_weights = [piece.reshape(-1, model_width) for piece in down]

    back = [("y", "x"), ("x", "y"), ("l", "l"), ("h", "h")]

    def give_all(pieces, names, axes):
        pairs = [halves_at(piece, bits[name], axis[name]) for piece, name, axis in zip(pieces, names, axes)]
        return [pair[0] for pair in pairs], swap_all([pair[1] for pair in pairs], names)

    def add_all(kept, got):
        return [(a.astype(f32) + b.astype(f32)).astype(low) for a, b in zip(kept, got)]

    down_back = [whole.reshape(2, 2, 2, 2, -1, model_width) for whole in down_grads]
    kept_d, got_d = give_all(down_back, back[0], downs)
    pre_grads, unit_sums = [], []
    for at in range(2):
        act_grad = project("bsd,kd->bsk", branch_grad, down_weights[at])
        pre_grads.append((act_grad * slopes[at].astype(f32)).astype(low))
        unit_sums.append(jnp.sum(pre_grads[at], axis=(0, 1), dtype=f32))
    mid_part = sum(project("bsk,dk->bsd", pre_grads[at], up_weights[at]) for at in range(2)).astype(low)
    kept_d, got_d, pre_grads, mid_part = tie((kept_d, got_d, pre_grads, mid_part))
    down_back = add_all(kept_d, got_d)

    mid_other = partner_swap(mid_part, "c")
    kept_d, got_d = give_all(down_back, back[1], downs)
    up_grads = [project("bsd,bsk->dk", mlp_in, pre_grad).astype(low) for pre_grad in pre_grads]
    kept_d, got_d, up_grads, mid_other = tie((kept_d, got_d, up_grads, mid_other))
    down_back = add_all(kept_d, got_d)

    up_back = [whole.reshape(2, 2, 2, 2 * rows_here, -1) for whole in up_grads]
    kept_d, got_d = give_all(down_back, back[2], downs)
    kept_u, got_u = give_all(up_back, back[0], ups)
    attn_grad, mid_sums = row_calls(
        norm_back_body(2, True), [mid_part, mid_other, hidden, branch_grad], [norm_vec], [low], 3
    )
    mixed_grad = project("bsd,kd->bsk", attn_grad, out_weight).astype(low)
    out_grad = project("bsk,bsd->kd", mixed_low, attn_grad).astype(low)
    mlp_part = sum(project("bsk,kd->bsd", act_vals[at], down_weights[at]) for at in range(2)).astype(low)
    kept_d, got_d, kept_u, got_u, mixed_grad, out_grad, mlp_part, attn_grad, mid_sums = tie(
        (kept_d, got_d, kept_u, got_u, mixed_grad, out_grad, mlp_part, attn_grad, mid_sums)
    )
    down_back = add_all(kept_d, got_d)
    up_back = add_all(kept_u, got_u)

    kept_d, got_d = give_all(down_back, back[3], downs)
    kept_u, got_u = give_all(up_back, back[1], ups)
    out_back = [out_grad.reshape(2, 2, 2, 2 * out_rows, model_width)]
    kept_o, got_o = give_all(out_back, "y", [out_axes])
    mlp_other = partner_swap(mlp_part, "c")
    first_half = attend_back(queries, key_vecs, values, mixed_grad, level, 0, 2)
    kept_d, got_d, kept_u, got_u, kept_o, got_o, mlp_other, first_half, mixed_grad = tie(
        (kept_d, got_d, kept_u, got_u, kept_o, got_o, mlp_other, first_half, mixed_grad)
    )
    down_back = add_all(kept_d, got_d)
    up_back = add_all(kept_u, got_u)
    out_back = add_all(kept_o, got_o)
    result = (
        hidden + (mlp_part.astype(f32) + mlp_other.astype(f32) + norm_vec[5])
    ).astype(low)
    result_other = to_owner(result)

    def qkv_products(half):
        return [
            project("bsd,bse->de", attn_in, grad).astype(low).reshape(1, 2, 2, 2, 2 * rows_here, -1)
            for grad in half
        ]

    thirds = [qkv_axes] * 3
    qkv_back = [("y", "x", "y"), ("x", "y", "x"), ("l",) * 3, ("h",) * 3]
    first_back = qkv_products(first_half)
    kept_q, got_q = give_all(first_back, qkv_back[0], thirds)
    kept_u, got_u = give_all(up_back, back[2], ups)
    kept_o, got_o = give_all(out_back, "x", [out_axes])
    second_half = attend_back(queries, key_vecs, values, mixed_grad, level, 1, 2)
    kept_q, got_q, kept_u, got_u, kept_o, got_o, second_half = tie(
        (kept_q, got_q, kept_u, got_u, kept_o, got_o, second_half)
    )
    first_back = add_all(kept_q, got_q)
    up_back = add_all(kept_u, got_u)
    out_back = add_all(kept_o, got_o)

    kept_q, got_q = give_all(first_back, qkv_back[1], thirds)
    kept_u, got_u = give_all(up_back, back[3], ups)
    kept_o, got_o = give_all(out_back, "l", [out_axes])
    second_back = qkv_products(second_half)
    kept_s, got_s = give_all(second_back, qkv_back[0], thirds)

    def rejoined(one, two):
        cut = half_width // 2
        return jnp.concatenate(
            [one[..., :cut], two[..., :cut], one[..., cut:], two[..., cut:]], axis=-1
        )

    query_grad, key_grad, value_grad = (rejoined(a, b) for a, b in zip(first_half, second_half))
    in_part = (
        project("bse,de->bsd", query_grad, qk_weight[0])
        + project("bse,de->bsd", key_grad, qk_weight[1])
        + project("bse,de->bsd", value_grad, v_weight)
    ).astype(low)
    in_other = partner_swap(in_part, "c")
    input_low, in_sums = row_calls(
        norm_back_body(0, False), [in_part, in_other, tokens, attn_grad], [norm_vec], [low], 2
    )
    kept_q, got_q, kept_u, got_u, kept_o, got_o, input_low, in_sums = tie(
        (kept_q, got_q, kept_u, got_u, kept_o, got_o, input_low, in_sums)
    )
    input_other = to_owner(input_low)
    first_back = add_all(kept_q, got_q)
    up_back = add_all(kept_u, got_u)
    out_back = add_all(kept_o, got_o)

    norm_rows = jnp.concatenate(
        [in_sums, mid_sums, jnp.sum(branch_grad, axis=(0, 1), dtype=f32)[None]]
    )
    norm_rows = jnp.where(core == 0, norm_rows, 0.0)
    head_sums = jnp.stack(
        [jnp.sum(query_grad, axis=(0, 1), dtype=f32), jnp.sum(value_grad, axis=(0, 1), dtype=f32)]
    ).reshape(2, 2, half_width)
    unit_rows_sum = jnp.stack(unit_sums).reshape(2, 2, width)
    inner_rows = jnp.zeros((2 + unit_rows, 2, width), f32)
    inner_rows = lax.dynamic_update_slice(inner_rows, head_sums, (0, 0, core * half_width))
    inner_rows = lax.dynamic_update_slice(inner_rows, unit_rows_sum, (2 + core * 2, 0, 0))
    small_sums = jnp.concatenate([norm_rows, inner_rows.reshape(-1, model_width)])

    kept_s2, got_s2 = None, None
    second_back = add_all(kept_s, got_s)
    small_sums = small_sums + partner_swap(small_sums, "c")
    kept_q, got_q = give_all(first_back, qkv_back[2], thirds)
    kept_s, got_s = give_all(second_back, qkv_back[1], thirds)
    small_sums = small_sums + partner_swap(small_sums, "y")
    first_back, second_back = add_all(kept_q, got_q), add_all(kept_s, got_s)
    kept_q, got_q = give_all(first_back, qkv_back[3], thirds)
    kept_s, got_s = give_all(second_back, qkv_back[2], thirds)
    small_sums = small_sums + partner_swap(small_sums, "x")
    first_back, second_back = add_all(kept_q, got_q), add_all(kept_s, got_s)
    kept_s, got_s = give_all(second_back, qkv_back[3], thirds)
    small_sums = small_sums + partner_swap(small_sums, "l")
    second_back = add_all(kept_s, got_s)
    small_sums = small_sums + partner_swap(small_sums, "h")

    (out_part,) = out_back
    out_part = out_part[0, 0, 0]
    out_total = (out_part.astype(f32) + partner_swap(out_part, "h").astype(f32)).astype(low)
    keep, give = halves_at(out_total, core, 0)
    out_share = jnp.where(bits["h"] == core, keep, partner_swap(give, "c")).astype(f32)
    up_back = add_all(kept_u, got_u)
    keep, give = halves_at(jnp.stack([piece[0, 0, 0, 0] for piece in down_back]), core, 1)
    down_share = joined(keep, partner_swap(give, "c"), core, 0).astype(f32)
    keep, give = halves_at(jnp.stack([piece[0, 0, 0] for piece in up_back]), core, 1)
    up_share = joined(keep, partner_swap(give, "c"), core, 0).transpose(1, 0, 2).astype(f32)
    qkv_whole = jnp.concatenate(
        [
            jnp.concatenate([one[:, 0, 0, 0], two_[:, 0, 0, 0]], axis=-1)
            for one, two_ in zip(first_back, second_back)
        ]
    )
    keep, give = halves_at(qkv_whole, core, 1)
    qkv_share = joined(keep, partner_swap(give, "c"), core, -1).astype(f32)

    outputs = jnp.where(at_home, result, result_other)
    input_grad = jnp.where(at_home, input_low, input_other).astype(f32)
    place = lax.axis_index("dp")
    norm_share = lax.dynamic_slice_in_dim(small_sums[:6], place * rows_here, rows_here, 1)
    inner_share = lax.dynamic_slice_in_dim(small_sums[6:], tens * width + place * out_rows, out_rows, 1)

    qkv_new = adam_update(qkv_master, qkv_first, qkv_second, qkv_share, LEARN_RATES[0])
    out_new = adam_update(out_master, out_first, out_second, out_share, LEARN_RATES[1])
    up_new = adam_update(up_master, up_first, up_second, up_share, LEARN_RATES[2])
    down_new = adam_update(down_master, down_first, down_second, down_share, LEARN_RATES[3])
    norm_new = adam_update(norm_master, norm_first, norm_second, norm_share, LEARN_RATES[4])
    inner_new = adam_update(inner_master, inner_first, inner_second, inner_share, LEARN_RATES[5])
    return (outputs, input_grad, *qkv_new, *out_new, *up_new, *down_new, *norm_new, *inner_new)


def solution(mesh):
    placed = (
        P("dp", None, None),
        P("dp", None, None),
        P("dp"),
        P(None, "dp", "tensor"),
        P(None, "dp", "tensor"),
        P(None, "dp", "tensor"),
        P(("tensor", "dp"), None),
        P(("tensor", "dp"), None),
        P(("tensor", "dp"), None),
        P("dp", None, "tensor"),
        P("dp", None, "tensor"),
        P("dp", None, "tensor"),
        P(None, ("tensor", "dp"), None),
        P(None, ("tensor", "dp"), None),
        P(None, ("tensor", "dp"), None),
        P(None, "dp"),
        P(None, "dp"),
        P(None, "dp"),
        P(None, ("tensor", "dp")),
        P(None, ("tensor", "dp")),
        P(None, ("tensor", "dp")),
    )
    chip_pairs = mesh.shape["tensor"] == 2 and mesh.shape["dp"] == 16
    return jax.shard_map(
        on_chip_pair if chip_pairs else on_device,
        mesh=mesh,
        in_specs=placed,
        out_specs=(
            P("dp", None, None),
            P("dp", None, None),
            P(None, "dp", "tensor"),
            P(None, "dp", "tensor"),
            P(None, "dp", "tensor"),
            P(None, "dp", "tensor"),
            P(("tensor", "dp"), None),
            P(("tensor", "dp"), None),
            P(("tensor", "dp"), None),
            P(("tensor", "dp"), None),
            P("dp", None, "tensor"),
            P("dp", None, "tensor"),
            P("dp", None, "tensor"),
            P("dp", None, "tensor"),
            P(None, ("tensor", "dp"), None),
            P(None, ("tensor", "dp"), None),
            P(None, ("tensor", "dp"), None),
            P(None, ("tensor", "dp"), None),
            P(None, "dp"),
            P(None, "dp"),
            P(None, "dp"),
            P(None, "dp"),
            P(None, ("tensor", "dp")),
            P(None, ("tensor", "dp")),
            P(None, ("tensor", "dp")),
            P(None, ("tensor", "dp")),
        ),
        check_vma=False,
    )
```
